32 devices in a mesh: grp: 2 (over y), res: 8 (over z, x), seq: 2 (over core).
Axes of the slice: x: 2, y: 2, z: 4, core: 2. Of those that a mesh axis runs over, the one named last changes fastest.
Arguments:
- aligned_activity: bfloat16 [512, 512, 256], P(('grp', 'seq'), 'res'), parts along dimension 0, may hold values from -6 to 6
- pair_state: bfloat16 [1024, 512, 128], P(('grp', 'res'), 'seq'), parts along dimension 0, may hold values from -6 to 6
- focus_scaling_vector: float32 [256], replicated, may hold values from 0.5 to 2
- combined_probe_matrix: bfloat16 [256, 1024], replicated, may hold values from -0.375 to 0.375
- sigmoid_offset_vector: float32 [256], replicated, may hold values from -4 to 4
- focus_final_matrix: bfloat16 [256, 256], replicated, may hold values from -0.375 to 0.375
- pair_norm_gain: float32 [128], replicated, may hold values from 0.5 to 2
- pair_bias_matrix: float32 [128, 8], replicated, may hold values from -36 to 36
- feedforward_scaling_vector: float32 [256], replicated, may hold values from 0.5 to 2
- feedforward_widen_matrix: bfloat16 [256, 1024], replicated, may hold values from -0.375 to 0.375
- feedforward_shrink_matrix: bfloat16 [1024, 256], replicated, may hold values from -0.1875 to 0.1875
- tensor_scaling_vector: float32 [256], replicated, may hold values from 0.5 to 2
- twin_operand_matrix: bfloat16 [256, 64], replicated, may hold values from -0.375 to 0.375
- tensor_final_matrix: bfloat16 [1024, 128], replicated, may hold values from -3 to 3
Outputs:
- alignment_output: bfloat16 [512, 512, 256], P(('grp', 'seq'), 'res'), parts along dimension 0
- pair_output: bfloat16 [1024, 512, 128], P(('grp', 'res'), 'seq'), parts along dimension 0
The draws below stay inside these ranges and needn't reach their ends.
There are 2 independent parts, one for each index of `grp`. The reference program is written for one: setup_inputs(seed, part) draws one part's arguments, and reference() takes and returns one part's arrays. A program takes and returns all parts, laid end to end along the dimension named above; an argument that names none is the same for every part. Nothing has to cross between parts.
All inputs are finite; a program needn't handle non-finite values.
Results may differ from the reference program's by a relative error of at most 0.0095.
The reference program's roundings to bfloat16 on the way count: a program that leaves them out, or rounds other values in their place, can miss the bound.
Values may be sent and summed in bfloat16 or wider, within the bound.
No kernel may reach another device: no remote copies, remote signals or barrier semaphores. Data moves between devices by JAX's collectives and lax.ppermute only.
A program may use at most 256 MiB of HBM per device.

```python
import math
import jax
import jax.numpy as jnp
from jax import lax

ALIGNED_DEPTH = 256
COUPLING_DEPTH = 128
FOCUS_GROUPS = 8
PRODUCT_DEPTH = 32
ALIGNED_CHAINS = 256
AMINO_SITES = 512
HIDDEN_UNITS = 1024
N_RES = 8


def draw_pair_bias_matrix(key, part):
    raw = jnp.clip(jax.random.normal(key, (COUPLING_DEPTH, FOCUS_GROUPS), jnp.float32), -4.0, 4.0)
    return raw * 0.09


def level_of(rng, shape, split, low, largest):
    gain = 1.0
    for position, parts in split:
        steps = jax.random.uniform(jax.random.fold_in(jax.random.fold_in(rng, 6), position), (parts,), jnp.float32, low / len(split), largest / len(split))
        gain = gain * jnp.repeat(jnp.exp(steps), shape[position] // parts).reshape((-1,) + (1,) * (len(shape) - 1 - position))
    return gain


def normal_values(own_key, extent, width, reach, split=(), held_as=jnp.bfloat16):
    entries = jax.random.normal(own_key, extent, jnp.float32) * width
    if len(split) > 0:
        entries = level_of(own_key, extent, split, -0.22, 0.18) * entries
    return jnp.clip(entries, min=-reach, max=reach).astype(held_as)


def setup_inputs(seed: int = 0, part: int = 0) -> dict:
    splits = jax.random.split(jax.random.key(seed), 15)
    own_keys = jax.random.split(jax.random.fold_in(splits[14], part), 15)
    aligned_activity = normal_values(own_keys[0], (ALIGNED_CHAINS, AMINO_SITES, ALIGNED_DEPTH), 1.0, 6.0, ((0, 2), (1, 8)))
    pair_state = normal_values(own_keys[1], (AMINO_SITES, AMINO_SITES, COUPLING_DEPTH), 1.0, 6.0, ((0, 8), (1, 2)))
    focus_scaling_vector = jnp.clip(jnp.exp(jax.random.uniform(splits[2], (ALIGNED_DEPTH,), jnp.float32, math.log(0.5), math.log(2.0))), 0.5, 2.0)
    combined_probe_matrix = normal_values(splits[3], (ALIGNED_DEPTH, 4 * ALIGNED_DEPTH), ALIGNED_DEPTH ** -0.5, 0.375)
    sigmoid_offset_vector = normal_values(splits[4], (ALIGNED_DEPTH,), 1.0, 4.0, (), jnp.float32)
    focus_final_matrix = normal_values(splits[5], (ALIGNED_DEPTH, ALIGNED_DEPTH), ALIGNED_DEPTH ** -0.5, 0.375)
    pair_norm_gain = jnp.clip(jnp.exp(jax.random.uniform(splits[6], (COUPLING_DEPTH,), jnp.float32, math.log(0.5), math.log(2.0))), 0.5, 2.0)
    pair_bias_matrix = draw_pair_bias_matrix(jax.random.fold_in(splits[14], 71), part)
    feedforward_scaling_vector = jnp.clip(jnp.exp(jax.random.uniform(splits[8], (ALIGNED_DEPTH,), jnp.float32, math.log(0.5), math.log(2.0))), 0.5, 2.0)
    feedforward_widen_matrix = normal_values(splits[9], (ALIGNED_DEPTH, HIDDEN_UNITS), ALIGNED_DEPTH ** -0.5, 0.375)
    feedforward_shrink_matrix = normal_values(splits[10], (HIDDEN_UNITS, ALIGNED_DEPTH), HIDDEN_UNITS ** -0.5, 0.1875)
    tensor_scaling_vector = jnp.clip(jnp.exp(jax.random.uniform(splits[11], (ALIGNED_DEPTH,), jnp.float32, math.log(0.5), math.log(2.0))), 0.5, 2.0)
    twin_operand_matrix = normal_values(splits[12], (ALIGNED_DEPTH, 2 * PRODUCT_DEPTH), ALIGNED_DEPTH ** -0.5, 0.375)
    tensor_final_matrix = normal_values(splits[13], (PRODUCT_DEPTH * PRODUCT_DEPTH, COUPLING_DEPTH), (max(1, PRODUCT_DEPTH * PRODUCT_DEPTH // ALIGNED_CHAINS)) ** -0.5, 3.0)
    return dict(aligned_activity=aligned_activity, pair_state=pair_state, focus_scaling_vector=focus_scaling_vector, combined_probe_matrix=combined_probe_matrix, sigmoid_offset_vector=sigmoid_offset_vector, focus_final_matrix=focus_final_matrix, pair_norm_gain=pair_norm_gain, pair_bias_matrix=pair_bias_matrix, feedforward_scaling_vector=feedforward_scaling_vector, feedforward_widen_matrix=feedforward_widen_matrix, feedforward_shrink_matrix=feedforward_shrink_matrix, tensor_scaling_vector=tensor_scaling_vector, twin_operand_matrix=twin_operand_matrix, tensor_final_matrix=tensor_final_matrix)


def layer_normalize(inputs, scale_gain):
    sample_expectation = lax.optimization_barrier(jnp.mean(inputs, axis=-1, keepdims=True))
    centered = inputs - sample_expectation
    variance = lax.optimization_barrier(jnp.mean(centered * centered, axis=-1, keepdims=True))
    return centered * lax.rsqrt(variance + 1e-05) * scale_gain

def reference(aligned_activity, pair_state, focus_scaling_vector, combined_probe_matrix, sigmoid_offset_vector, focus_final_matrix, pair_norm_gain, pair_bias_matrix, feedforward_scaling_vector, feedforward_widen_matrix, feedforward_shrink_matrix, tensor_scaling_vector, twin_operand_matrix, tensor_final_matrix):
    subspace_depth = ALIGNED_DEPTH // FOCUS_GROUPS
    probe_multiplier = subspace_depth ** (-0.5)
    pair_norm = layer_normalize(pair_state.astype(jnp.float32), pair_norm_gain)
    pair_bias = jnp.einsum('ijc,ch->hij', pair_norm, pair_bias_matrix, precision=lax.Precision.HIGHEST).astype(jnp.bfloat16)
    bias_wide = pair_bias.astype(jnp.float32)

    def row_attention_update(sequence):
        residual_state = sequence.astype(jnp.float32)
        normalized_rows = layer_normalize(residual_state, focus_scaling_vector).astype(jnp.bfloat16)
        mapped_entries = jnp.dot(normalized_rows, combined_probe_matrix, preferred_element_type=jnp.float32)
        probe_entries = (mapped_entries[:, :ALIGNED_DEPTH] * probe_multiplier).astype(jnp.bfloat16).reshape(AMINO_SITES, FOCUS_GROUPS, subspace_depth)
        lookup_entries = mapped_entries[:, ALIGNED_DEPTH:2 * ALIGNED_DEPTH].astype(jnp.bfloat16).reshape(AMINO_SITES, FOCUS_GROUPS, subspace_depth)
        content_entries = mapped_entries[:, 2 * ALIGNED_DEPTH:3 * ALIGNED_DEPTH].astype(jnp.bfloat16).reshape(AMINO_SITES, FOCUS_GROUPS, subspace_depth)
        sigmoid_filter = jax.nn.sigmoid(mapped_entries[:, 3 * ALIGNED_DEPTH:] + sigmoid_offset_vector)
        scores = jnp.einsum('ihd,jhd->hij', probe_entries.astype(jnp.float32), lookup_entries.astype(jnp.float32)) + bias_wide
        top_score = lax.optimization_barrier(jnp.max(scores, axis=-1, keepdims=True))
        exponent = jnp.exp(scores - top_score)
        softmax_shares = (exponent / lax.optimization_barrier(jnp.sum(exponent, axis=-1, keepdims=True))).astype(jnp.bfloat16)
        mixed_entries = jnp.einsum('tnx,xtq->ntq', softmax_shares.astype(jnp.float32), content_entries.astype(jnp.float32)).reshape(AMINO_SITES, ALIGNED_DEPTH)
        gated_rows = (mixed_entries * sigmoid_filter).astype(jnp.bfloat16)
        residual_state = residual_state + jnp.dot(gated_rows, focus_final_matrix, preferred_element_type=jnp.float32)
        normalized_rows = layer_normalize(residual_state, feedforward_scaling_vector).astype(jnp.bfloat16)
        hidden = jnp.maximum(jnp.dot(normalized_rows, feedforward_widen_matrix, preferred_element_type=jnp.float32), 0.0).astype(jnp.bfloat16)
        residual_state = residual_state + jnp.dot(hidden, feedforward_shrink_matrix, preferred_element_type=jnp.float32)
        updated_state = residual_state.astype(jnp.bfloat16)
        normalized_rows = layer_normalize(updated_state.astype(jnp.float32), tensor_scaling_vector).astype(jnp.bfloat16)
        left_right_factors = jnp.dot(normalized_rows, twin_operand_matrix, preferred_element_type=jnp.float32).astype(jnp.bfloat16)
        return (updated_state, left_right_factors)
    alignment_output, left_right_factors = lax.map(row_attention_update, aligned_activity)
    left_fac = left_right_factors[:, :, :PRODUCT_DEPTH].astype(jnp.float32)
    right_fac = left_right_factors[:, :, PRODUCT_DEPTH:].astype(jnp.float32)
    row_block = AMINO_SITES // N_RES
    out_table = tensor_final_matrix.astype(jnp.float32).reshape(PRODUCT_DEPTH, PRODUCT_DEPTH, COUPLING_DEPTH)

    def pair_rows(block_index):
        left_rows = lax.dynamic_slice_in_dim(left_fac, block_index * row_block, row_block, 1)
        tensor_total = jnp.einsum('sic,sje->icje', left_rows, right_fac, precision=lax.Precision.HIGHEST)
        sample_expectation = (tensor_total / ALIGNED_CHAINS).astype(jnp.bfloat16)
        return jnp.einsum('icje,cez->ijz', sample_expectation.astype(jnp.float32), out_table, precision=lax.Precision.HIGHEST)
    update = lax.map(pair_rows, jnp.arange(N_RES, dtype=jnp.int32)).reshape(AMINO_SITES, AMINO_SITES, COUPLING_DEPTH)
    pair_output = (pair_state.astype(jnp.float32) + update).astype(jnp.bfloat16)
    return (alignment_output, pair_output)
```

```python
import functools
import math

import jax
import jax.numpy as jnp
from jax import lax
from jax.experimental import pallas as pl
from jax.experimental.pallas import tpu as pltpu
from jax.sharding import PartitionSpec as P

CHUNKS = 2
VMEM_BYTES = 56 * 2**20
F32 = jnp.float32
BF16 = jnp.bfloat16
ROWS_BY_ROWS = (((1,), (1,)), ((), ()))


def layer_normalize(inputs, scale_gain):
    sample_expectation = jnp.mean(inputs, axis=-1, keepdims=True)
    centered = inputs - sample_expectation
    variance = jnp.mean(centered * centered, axis=-1, keepdims=True)
    return centered * lax.rsqrt(variance + 1e-05) * scale_gain


def attend_kernel(
    heads,
    x_ref,
    bias_ref,
    gain1_ref,
    probe_ref,
    offset_ref,
    final_ref,
    gain2_ref,
    widen_ref,
    shrink_ref,
    gain3_ref,
    twin_ref,
    out_ref,
    left_ref,
    right_ref,
    q_ref,
    k_ref,
    v_ref,
    mixed_ref,
):
    blocks, _, block_rows, width = x_ref.shape
    length = blocks * block_rows
    depth = width // heads
    x = x_ref[:, 0].reshape(length, width).astype(F32)
    normed = layer_normalize(x, gain1_ref[...]).astype(BF16)

    def project(part):
        return jnp.dot(
            normed, probe_ref[:, part * width : (part + 1) * width], preferred_element_type=F32
        )

    q_ref[...] = (project(0) * depth**-0.5).astype(BF16)
    k_ref[...] = project(1).astype(BF16)
    v_ref[...] = project(2).astype(BF16)
    gate = jax.nn.sigmoid(project(3) + offset_ref[...])
    halves = bias_ref.shape[0]
    half = length // halves
    lane_head = lax.broadcasted_iota(jnp.int32, (1, width), 1) // depth
    for h in range(heads):
        own = (lane_head == h).astype(F32).astype(BF16)
        scores = lax.dot_general(
            q_ref[...], k_ref[...] * own, ROWS_BY_ROWS, preferred_element_type=F32
        )
        bias = jnp.concatenate(
            [bias_ref[j, :, h].reshape(length, half) for j in range(halves)], axis=1
        )
        scores = scores + bias.astype(F32)
        exponent = jnp.exp(scores - jnp.max(scores, axis=-1, keepdims=True))
        denominator = jnp.sum(exponent, axis=-1, keepdims=True)
        shares = (exponent * (1.0 / denominator)).astype(BF16)
        mixed = jnp.dot(shares, v_ref[...] * own, preferred_element_type=F32)
        if h == 0:
            mixed_ref[...] = mixed
        else:
            mixed_ref[...] += mixed
    gated = (mixed_ref[...] * gate).astype(BF16)
    stream = x + jnp.dot(gated, final_ref[...], preferred_element_type=F32)
    normed = layer_normalize(stream, gain2_ref[...]).astype(BF16)
    hidden = jnp.maximum(
        jnp.dot(normed, widen_ref[...], preferred_element_type=F32), 0.0
    ).astype(BF16)
    updated = (stream + jnp.dot(hidden, shrink_ref[...], preferred_element_type=F32)).astype(BF16)
    out_ref[:, 0] = updated.reshape(blocks, block_rows, width)
    normed = layer_normalize(updated.astype(F32), gain3_ref[...]).astype(BF16)
    factors = lax.dot_general(
        twin_ref[...], normed, ROWS_BY_ROWS, preferred_element_type=F32
    ).astype(BF16)
    factor_width = factors.shape[0] // 2
    left_ref[0] = factors[:factor_width]
    for j in range(halves):
        right_ref[j, 0] = factors[factor_width:, j * half : (j + 1) * half]


def attend(x, bias, params, heads):
    blocks, seqs, block_rows, width = x.shape
    length = blocks * block_rows
    halves = bias.shape[0]
    half = length // halves
    factor_width = params[-1].shape[0] // 2
    hidden = params[5].shape[1]
    held = (bias,) + params

    def whole(array):
        return pl.BlockSpec(array.shape, lambda s: (0,) * array.ndim)

    flops = seqs * (
        2 * length * width * (5 * width + 2 * hidden + 2 * factor_width)
        + 4 * heads * length * length * width
    )
    rows = pl.BlockSpec((blocks, 1, block_rows, width), lambda s: (0, s, 0, 0))
    return pl.pallas_call(
        functools.partial(attend_kernel, heads),
        grid=(seqs,),
        in_specs=[rows] + [whole(array) for array in held],
        out_specs=[
            rows,
            pl.BlockSpec((1, factor_width, length), lambda s: (s, 0, 0)),
            pl.BlockSpec((halves, 1, factor_width, half), lambda s: (0, s, 0, 0)),
        ],
        out_shape=[
            jax.ShapeDtypeStruct(x.shape, BF16),
            jax.ShapeDtypeStruct((seqs, factor_width, length), BF16),
            jax.ShapeDtypeStruct((halves, seqs, factor_width, half), BF16),
        ],
        scratch_shapes=[pltpu.VMEM((length, width), BF16)] * 3
        + [pltpu.VMEM((length, width), F32)],
        compiler_params=pltpu.CompilerParams(vmem_limit_bytes=VMEM_BYTES),
        cost_estimate=pl.CostEstimate(
            flops=flops,
            bytes_accessed=4 * x.size + 2 * bias.size,
            transcendentals=seqs * heads * length * length,
        ),
        name="attend",
    )(x, *held)


def outer_kernel(rows, seq_total, left_ref, right_ref, final_ref, pair_ref, out_ref, mean_ref):
    width = right_ref.shape[0]
    left = left_ref[...]
    for e in range(width):
        outer = jnp.dot(left, right_ref[e], preferred_element_type=F32).astype(BF16)
        mean_ref[:, e * width : (e + 1) * width, :] = outer.reshape(rows, width, -1)
    final = final_ref[...]
    for i in range(rows):
        update = jnp.dot(final, mean_ref[i], preferred_element_type=F32)
        out_ref[i] = (pair_ref[i].astype(F32) + update.T * (1.0 / seq_total)).astype(BF16)


def outer_update(left, right, final, pair_state):
    width, seqs, cols = right.shape
    row_count, _, channels = pair_state.shape
    rows = math.gcd(row_count, 16)

    def whole(array):
        return pl.BlockSpec(array.shape, lambda i: (0,) * array.ndim)

    block = pl.BlockSpec((rows, cols, channels), lambda i: (i, 0, 0))
    return pl.pallas_call(
        functools.partial(outer_kernel, rows, float(seqs)),
        grid=(row_count // rows,),
        in_specs=[
            pl.BlockSpec((rows * width, seqs), lambda i: (i, 0)),
            whole(right),
            whole(final),
            block,
        ],
        out_specs=block,
        out_shape=jax.ShapeDtypeStruct(pair_state.shape, BF16),
        scratch_shapes=[pltpu.VMEM((rows, width * width, cols), BF16)],
        compiler_params=pltpu.CompilerParams(vmem_limit_bytes=VMEM_BYTES),
        cost_estimate=pl.CostEstimate(
            flops=2 * row_count * width * width * cols * (seqs + channels),
            bytes_accessed=2 * right.size + 4 * pair_state.size,
            transcendentals=0,
        ),
        name="outer_update",
    )(left, right, final, pair_state)


def on_device(
    aligned_activity,
    pair_state,
    focus_scaling_vector,
    combined_probe_matrix,
    sigmoid_offset_vector,
    focus_final_matrix,
    pair_norm_gain,
    pair_bias_matrix,
    feedforward_scaling_vector,
    feedforward_widen_matrix,
    feedforward_shrink_matrix,
    tensor_scaling_vector,
    twin_operand_matrix,
    tensor_final_matrix,
):
    heads = pair_bias_matrix.shape[1]
    factor_width = twin_operand_matrix.shape[1] // 2
    channels = tensor_final_matrix.shape[1]
    seq_local, res_local, width = aligned_activity.shape
    blocks = lax.axis_size("res")
    chunks = math.gcd(seq_local // blocks, CHUNKS)
    chunk_seqs = seq_local // blocks // chunks

    arrivals = [
        lax.all_to_all(part.reshape(blocks, chunk_seqs, res_local, width), "res", 0, 0)
        for part in jnp.split(aligned_activity, chunks, axis=0)
    ]

    pair_norm = layer_normalize(pair_state.astype(F32), pair_norm_gain)
    bias_tile = jnp.einsum(
        "ijc,ch->hij", pair_norm, pair_bias_matrix, precision=lax.Precision.HIGHEST
    ).astype(BF16)
    bias = lax.all_gather(lax.all_gather(bias_tile, "res"), "seq")

    params = (
        focus_scaling_vector.reshape(1, -1),
        combined_probe_matrix,
        sigmoid_offset_vector.reshape(1, -1),
        focus_final_matrix,
        feedforward_scaling_vector.reshape(1, -1),
        feedforward_widen_matrix,
        feedforward_shrink_matrix,
        tensor_scaling_vector.reshape(1, -1),
        twin_operand_matrix.T,
    )
    outputs, lefts, rights = [], [], []
    for x in arrivals:
        updated, left, right = attend(x, bias, params, heads)
        outputs.append(
            lax.all_to_all(updated, "res", 0, 0).reshape(-1, res_local, width)
        )
        left = left.reshape(chunk_seqs, factor_width, blocks, res_local)
        left = left.transpose(2, 0, 1, 3).reshape(blocks, chunk_seqs, -1)
        left = lax.all_gather(lax.all_to_all(left, "res", 0, 0), "seq")
        lefts.append(left.reshape(-1, blocks, chunk_seqs, factor_width, res_local))
        right = lax.all_gather(lax.all_to_all(right, "seq", 0, 0), "res")
        rights.append(right)

    left = jnp.stack(lefts).transpose(5, 4, 0, 2, 1, 3)
    left = left.reshape(res_local * factor_width, -1)
    right = jnp.stack(rights).transpose(4, 0, 1, 2, 3, 5)
    right = right.reshape(factor_width, left.shape[1], -1)
    final = tensor_final_matrix.reshape(factor_width, factor_width, channels)
    final = final.transpose(2, 1, 0).reshape(channels, -1)
    pair_output = outer_update(left, right, final, pair_state)
    return (jnp.concatenate(outputs, axis=0), pair_output)


def solution(mesh):
    return jax.shard_map(
        on_device,
        mesh=mesh,
        in_specs=(
            P(("grp", "seq"), "res", None),
            P(("grp", "res"), "seq", None),
        )
        + (P(),) * 12,
        out_specs=(P(("grp", "seq"), "res", None), P(("grp", "res"), "seq", None)),
        check_vma=False,
    )
```

```python
import functools
import math

import jax
import jax.numpy as jnp
from jax import lax
from jax.experimental import pallas as pl
from jax.experimental.pallas import tpu as pltpu
from jax.sharding import PartitionSpec as P

CHUNKS = 4
NEAR = 2
VMEM_BYTES = 56 * 2**20
F32 = jnp.float32
BF16 = jnp.bfloat16
ROWS_BY_ROWS = (((1,), (1,)), ((), ()))


def layer_normalize(inputs, scale_gain):
    sample_expectation = jnp.mean(inputs, axis=-1, keepdims=True)
    centered = inputs - sample_expectation
    variance = jnp.mean(centered * centered, axis=-1, keepdims=True)
    return centered * lax.rsqrt(variance + 1e-05) * scale_gain


def attend_kernel(heads, blocks, halves, place_ref, *refs):
    x_ref, refs = refs[0], refs[1:]
    biases, refs = refs[:halves], refs[halves:]
    (gain1_ref, probe_ref, offset_ref, final_ref, gain2_ref, widen_ref, shrink_ref) = refs[:7]
    (gain3_ref, twin_ref, out_ref, right_ref) = refs[7:11]
    (q_ref, k_ref, v_ref, mixed_ref) = refs[11:]
    _, _, block_rows, width = x_ref.shape
    length = blocks * block_rows
    depth = width // heads
    half = length // halves
    seq = place_ref[0]
    x = x_ref[:, 0].reshape(length, width).astype(F32)
    normed = layer_normalize(x, gain1_ref[...]).astype(BF16)

    def project(part):
        return jnp.dot(
            normed, probe_ref[:, part * width : (part + 1) * width], preferred_element_type=F32
        )

    q_ref[...] = (project(0) * depth**-0.5).astype(BF16)
    for held, part in ((k_ref, 1), (v_ref, 2)):
        rows = project(part).astype(BF16)
        for j in range(halves):
            slot = lax.rem(j + halves - seq, halves)
            held[slot] = rows[j * half : (j + 1) * half]
    gate = jax.nn.sigmoid(project(3) + offset_ref[...])
    lane_head = lax.broadcasted_iota(jnp.int32, (1, width), 1) // depth
    for h in range(heads):
        own = (lane_head == h).astype(F32).astype(BF16)
        keys = k_ref[...].reshape(length, width) * own
        values = v_ref[...].reshape(length, width) * own
        scores = lax.dot_general(q_ref[...], keys, ROWS_BY_ROWS, preferred_element_type=F32)
        bias = jnp.concatenate(
            [
                jnp.concatenate([b[place_ref[1 + p], h] for p in range(blocks)], axis=0)
                for b in biases
            ],
            axis=1,
        )
        scores = scores + bias.astype(F32)
        exponent = jnp.exp(scores - jnp.max(scores, axis=-1, keepdims=True))
        denominator = jnp.sum(exponent, axis=-1, keepdims=True)
        shares = (exponent * (1.0 / denominator)).astype(BF16)
        mixed = jnp.dot(shares, values, preferred_element_type=F32)
        if h == 0:
            mixed_ref[...] = mixed
        else:
            mixed_ref[...] += mixed
    gated = (mixed_ref[...] * gate).astype(BF16)
    stream = x + jnp.dot(gated, final_ref[...], preferred_element_type=F32)
    normed = layer_normalize(stream, gain2_ref[...]).astype(BF16)
    hidden = jnp.maximum(
        jnp.dot(normed, widen_ref[...], preferred_element_type=F32), 0.0
    ).astype(BF16)
    updated = (stream + jnp.dot(hidden, shrink_ref[...], preferred_element_type=F32)).astype(BF16)
    out_ref[:, 0] = updated.reshape(blocks, block_rows, width)
    normed = layer_normalize(updated.astype(F32), gain3_ref[...]).astype(BF16)
    factors = lax.dot_general(
        twin_ref[...], normed, ROWS_BY_ROWS, preferred_element_type=F32
    ).astype(BF16)
    for j in range(halves):
        right_ref[j, 0] = factors[:, j * half : (j + 1) * half]


def attend(place, x, first, seqs, biases, params, heads):
    halves = len(biases)
    blocks, _, block_rows, width = x.shape
    length = blocks * block_rows
    half = length // halves
    factor_width = params[-1].shape[0]
    hidden = params[5].shape[1]
    held = tuple(biases) + params

    def whole(array):
        return pl.BlockSpec(array.shape, lambda s, place: (0,) * array.ndim)

    flops = 2 * seqs * (
        2 * length * width * (5 * width + 2 * hidden + factor_width)
        + 4 * heads * length * length * width
    )
    block = (blocks, 1, block_rows, width)
    return pl.pallas_call(
        functools.partial(attend_kernel, heads, blocks, halves),
        grid_spec=pltpu.PrefetchScalarGridSpec(
            num_scalar_prefetch=1,
            grid=(seqs,),
            in_specs=[pl.BlockSpec(block, lambda s, place: (0, first + s, 0, 0))]
            + [whole(array) for array in held],
            out_specs=[
                pl.BlockSpec(block, lambda s, place: (0, s, 0, 0)),
                pl.BlockSpec((halves, 1, factor_width, half), lambda s, place: (0, s, 0, 0)),
            ],
            scratch_shapes=[
                pltpu.VMEM((length, width), BF16),
                pltpu.VMEM((halves, half, width), BF16),
                pltpu.VMEM((halves, half, width), BF16),
                pltpu.VMEM((length, width), F32),
            ],
        ),
        out_shape=[
            jax.ShapeDtypeStruct((blocks, seqs, block_rows, width), BF16),
            jax.ShapeDtypeStruct((halves, seqs, factor_width, half), BF16),
        ],
        compiler_params=pltpu.CompilerParams(vmem_limit_bytes=VMEM_BYTES),
        cost_estimate=pl.CostEstimate(
            flops=flops,
            bytes_accessed=4 * seqs * length * width + 2 * heads * length * length,
            transcendentals=seqs * heads * length * length,
        ),
        name="attend",
    )(place, x, *held)


def bias_kernel(pair_ref, gain_ref, matrix_ref, out_ref, held_ref):
    for i in range(pair_ref.shape[0]):
        normed = layer_normalize(pair_ref[i].astype(F32), gain_ref[...])
        held_ref[:, i, :] = lax.dot_general(
            matrix_ref[...],
            normed,
            ROWS_BY_ROWS,
            precision=lax.Precision.HIGHEST,
            preferred_element_type=F32,
        )
    out_ref[...] = held_ref[...].astype(BF16)


def head_biases(pair_state, gain, matrix):
    row_count, cols, channels = pair_state.shape
    heads = matrix.shape[1]
    rows = math.gcd(row_count, 16)
    return pl.pallas_call(
        bias_kernel,
        grid=(row_count // rows,),
        in_specs=[
            pl.BlockSpec((rows, cols, channels), lambda i: (i, 0, 0)),
            pl.BlockSpec((1, channels), lambda i: (0, 0)),
            pl.BlockSpec((heads, channels), lambda i: (0, 0)),
        ],
        out_specs=pl.BlockSpec((heads, rows, cols), lambda i: (0, i, 0)),
        out_shape=jax.ShapeDtypeStruct((heads, row_count, cols), BF16),
        scratch_shapes=[pltpu.VMEM((heads, rows, cols), F32)],
        compiler_params=pltpu.CompilerParams(vmem_limit_bytes=VMEM_BYTES),
        cost_estimate=pl.CostEstimate(
            flops=100 * pair_state.size, bytes_accessed=2 * pair_state.size, transcendentals=0
        ),
        name="head_biases",
    )(pair_state, gain.reshape(1, -1), matrix.T)


def left_kernel(place_ref, x_ref, gain_ref, twin_ref, out_ref):
    blocks, seqs, rows, width = x_ref.shape
    x = jnp.concatenate([x_ref[place_ref[k]] for k in range(blocks)], axis=0)
    normed = layer_normalize(x.reshape(blocks * seqs * rows, width).astype(F32), gain_ref[...])
    out_ref[...] = lax.dot_general(
        twin_ref[...], normed.astype(BF16), ROWS_BY_ROWS, preferred_element_type=F32
    ).astype(BF16)


def left_factors(origins, x, gain, twin):
    blocks, seqs, rows, width = x.shape

    def whole(array):
        return pl.BlockSpec(array.shape, lambda i, place: (0,) * array.ndim)

    total = blocks * seqs * rows
    return pl.pallas_call(
        left_kernel,
        grid_spec=pltpu.PrefetchScalarGridSpec(
            num_scalar_prefetch=1,
            grid=(1,),
            in_specs=[whole(x), whole(gain), whole(twin)],
            out_specs=pl.BlockSpec((twin.shape[0], total), lambda i, place: (0, 0)),
        ),
        out_shape=jax.ShapeDtypeStruct((twin.shape[0], total), BF16),
        compiler_params=pltpu.CompilerParams(vmem_limit_bytes=VMEM_BYTES),
        cost_estimate=pl.CostEstimate(
            flops=8 * x.size * twin.shape[0], bytes_accessed=2 * x.size, transcendentals=0
        ),
        name="left_factors",
    )(origins, x, gain, twin)


def outer_kernel(rows, seq_total, left_ref, right_ref, final_ref, pair_ref, out_ref, mean_ref):
    width = right_ref.shape[0]
    left = left_ref[...]
    for e in range(width):
        outer = jnp.dot(left, right_ref[e], preferred_element_type=F32).astype(BF16)
        mean_ref[:, e * width : (e + 1) * width, :] = outer.reshape(rows, width, -1)
    final = final_ref[...]
    for i in range(rows):
        update = jnp.dot(final, mean_ref[i], preferred_element_type=F32)
        out_ref[i] = (pair_ref[i].astype(F32) + update.T * (1.0 / seq_total)).astype(BF16)


def outer_update(left, right, final, pair_state):
    width, seqs, cols = right.shape
    row_count, _, channels = pair_state.shape
    rows = math.gcd(row_count, 16)

    def whole(array):
        return pl.BlockSpec(array.shape, lambda i: (0,) * array.ndim)

    block = pl.BlockSpec((rows, cols, channels), lambda i: (i, 0, 0))
    return pl.pallas_call(
        functools.partial(outer_kernel, rows, float(seqs)),
        grid=(row_count // rows,),
        in_specs=[
            pl.BlockSpec((rows * width, seqs), lambda i: (i, 0)),
            whole(right),
            whole(final),
            block,
        ],
        out_specs=block,
        out_shape=jax.ShapeDtypeStruct(pair_state.shape, BF16),
        scratch_shapes=[pltpu.VMEM((rows, width * width, cols), BF16)],
        compiler_params=pltpu.CompilerParams(vmem_limit_bytes=VMEM_BYTES),
        cost_estimate=pl.CostEstimate(
            flops=2 * row_count * width * width * cols * (seqs + channels),
            bytes_accessed=2 * right.size + 4 * pair_state.size,
            transcendentals=0,
        ),
        name="outer_update",
    )(left, right, final, pair_state)


def on_device(
    aligned_activity,
    pair_state,
    focus_scaling_vector,
    combined_probe_matrix,
    sigmoid_offset_vector,
    focus_final_matrix,
    pair_norm_gain,
    pair_bias_matrix,
    feedforward_scaling_vector,
    feedforward_widen_matrix,
    feedforward_shrink_matrix,
    tensor_scaling_vector,
    twin_operand_matrix,
    tensor_final_matrix,
):
    factor_width = twin_operand_matrix.shape[1] // 2
    heads = pair_bias_matrix.shape[1]
    channels = tensor_final_matrix.shape[1]
    seq_local, res_local, width = aligned_activity.shape
    blocks = lax.axis_size("res")
    halves = lax.axis_size("seq")
    res = lax.axis_index("res")
    seq = lax.axis_index("seq")
    chunks = math.gcd(seq_local // blocks, CHUNKS)
    seqs = seq_local // blocks // chunks
    joined = [1, chunks - 1] if chunks > 1 else [1]
    early = max(0, chunks - 2)
    near = math.gcd(blocks, NEAR)
    far = blocks // near

    def after(value, *done):
        return lax.optimization_barrier((value, done))[0]

    def from_cores(own, sent):
        return [own] + [
            lax.ppermute(sent(k), "seq", [(i, (i + k) % halves) for i in range(halves)])
            for k in range(1, halves)
        ]

    def far_gather(block):
        return [block] + [
            lax.ppermute(block, "res", [(i, (i + k * near) % blocks) for i in range(blocks)])
            for k in range(1, far)
        ]

    def near_gather(listed, each):
        lists = listed if each else [jnp.stack(listed)]
        for k in range(1, near):
            moves = [(i, i - i % near + (i + k) % near) for i in range(blocks)]
            lists = lists + [lax.ppermute(part, "res", moves) for part in lists]
        return jnp.stack(lists) if each else jnp.concatenate(lists)

    close, away = jnp.arange(near)[:, None], jnp.arange(far)[None, :]
    origins = (res // near - away) % far * near + (res % near - close) % near
    origins = origins.reshape(-1).astype(jnp.int32)
    p = jnp.arange(blocks)
    slots = (res % near - p % near) % near * far + (res // near - p // near) % far
    place = jnp.concatenate([seq.reshape(1), slots]).astype(jnp.int32)

    tile = head_biases(pair_state, pair_norm_gain, pair_bias_matrix)
    far_bias = far_gather(tile)
    arrivals, sources = [], []
    start = 0
    for size in joined:
        rows = blocks * seqs * size
        part = aligned_activity[start : start + rows]
        part = part.reshape(blocks, seqs * size, res_local, width)
        start += rows
        if arrivals:
            part = after(part, arrivals[-1], far_bias)
        arrivals.append(lax.all_to_all(part, "res", 0, 0))
        sources += [(len(arrivals) - 1, k * seqs) for k in range(size)]

    bias = after(near_gather(far_bias, True), arrivals[0])
    biases = from_cores(bias, lambda k: bias)
    biases = biases[:1] + biases[:0:-1]

    gain3 = tensor_scaling_vector.reshape(1, -1)
    params = (
        focus_scaling_vector.reshape(1, -1),
        combined_probe_matrix,
        sigmoid_offset_vector.reshape(1, -1),
        focus_final_matrix,
        feedforward_scaling_vector.reshape(1, -1),
        feedforward_widen_matrix,
        feedforward_shrink_matrix,
        gain3,
        twin_operand_matrix[:, factor_width:].T,
    )
    left_twin = twin_operand_matrix[:, :factor_width].T
    natural = jnp.arange(blocks, dtype=jnp.int32)
    outputs, lefts, rights, gathered, pending = [], [], [], [], None

    def swap(listed):
        def half_of(k):
            return lax.dynamic_index_in_dim(listed, lax.rem(seq + k, halves), 1, False)

        return jnp.stack(from_cores(half_of(0), half_of), axis=1)

    def finish(c):
        order = natural if c < early else origins
        left = left_factors(order, outputs[c], gain3, left_twin)
        left = left.reshape(factor_width, blocks, seqs, res_local)
        lefts.append(left.transpose(3, 0, 1, 2).reshape(res_local * factor_width, blocks, seqs))

    for c in range(chunks):
        done = []
        if c >= 1:
            done += [arrivals[-1]]
        if c >= 2:
            done += [outputs[c - 2]]
        if c >= 3:
            finish(c - 3)
            done += [lefts[c - 3]]
        source, first = sources[c]
        updated, right = attend(
            after(place, *done), arrivals[source], first, seqs, biases, params, heads
        )
        updated = after(updated, outputs[-1] if outputs else arrivals[-1])
        outputs.append(lax.all_to_all(updated, "res", 0, 0))
        rights.append(right)
        if c + 1 == early:
            gathered.append(lax.all_gather(jnp.concatenate(rights, axis=1), "res"))
        elif c >= early:
            if pending is not None:
                gathered.append(near_gather(after(pending, right), False))
            pending = far_gather(right)
    gathered.append(near_gather(pending, False))
    for c in range(max(0, chunks - 3), chunks):
        finish(c)

    rights = [swap(listed) for listed in gathered]
    right = jnp.concatenate([r.reshape(-1, *r.shape[3:]) for r in rights]).transpose(1, 0, 2)
    left = jnp.concatenate(lefts, axis=2)
    left = jnp.stack(from_cores(left, lambda k: left), axis=2)
    groups, start = [], 0
    for r in rights:
        part = left[..., start : start + r.shape[2]]
        start += r.shape[2]
        groups.append(part.reshape(res_local * factor_width, -1))
    left = jnp.concatenate(groups, axis=1)
    final = tensor_final_matrix.reshape(factor_width, factor_width, channels)
    final = final.transpose(2, 1, 0).reshape(channels, -1)
    pair_output = outer_update(left, right, final, pair_state)
    output = []
    for c in range(len(joined)):
        group = [outputs[k] for k, source in enumerate(sources) if source[0] == c]
        output.append(jnp.concatenate(group, axis=1).reshape(-1, res_local, width))
    output = jnp.concatenate(output)
    return (output, pair_output)


def solution(mesh):
    return jax.shard_map(
        on_device,
        mesh=mesh,
        in_specs=(
            P(("grp", "seq"), "res", None),
            P(("grp", "res"), "seq", None),
        )
        + (P(),) * 12,
        out_specs=(P(("grp", "seq"), "res", None), P(("grp", "res"), "seq", None)),
        check_vma=False,
    )
```

```python
import functools
import math

import jax
import jax.numpy as jnp
from jax import lax
from jax.experimental import pallas as pl
from jax.experimental.pallas import tpu as pltpu
from jax.sharding import PartitionSpec as P

CHUNKS = 4
NEAR = 2
VMEM_BYTES = 56 * 2**20
F32 = jnp.float32
BF16 = jnp.bfloat16
ROWS_BY_ROWS = (((1,), (1,)), ((), ()))


def layer_normalize(inputs, scale_gain):
    sample_expectation = jnp.mean(inputs, axis=-1, keepdims=True)
    centered = inputs - sample_expectation
    variance = jnp.mean(centered * centered, axis=-1, keepdims=True)
    return centered * lax.rsqrt(variance + 1e-05) * scale_gain


def attend_kernel(heads, blocks, halves, place_ref, *refs):
    x_ref, refs = refs[0], refs[1:]
    biases, refs = refs[:halves], refs[halves:]
    (gain1_ref, probe_ref, offset_ref, final_ref, gain2_ref, widen_ref, shrink_ref) = refs[:7]
    (gain3_ref, twin_ref, out_ref, right_ref) = refs[7:11]
    q_ref, k_ref, v_ref, *mixed_refs = refs[11:]
    _, _, block_rows, width = x_ref.shape
    length = blocks * block_rows
    depth = width // heads
    half = length // halves
    seq = place_ref[0]
    x = x_ref[:, 0].reshape(length, width).astype(F32)
    normed = layer_normalize(x, gain1_ref[...]).astype(BF16)

    def project(part):
        return jnp.dot(
            normed, probe_ref[:, part * width : (part + 1) * width], preferred_element_type=F32
        )

    q_ref[...] = (project(0) * depth**-0.5).astype(BF16)
    for held, part in ((k_ref, 1), (v_ref, 2)):
        rows = project(part).astype(BF16)
        for j in range(halves):
            slot = lax.rem(j + halves - seq, halves)
            held[slot] = rows[j * half : (j + 1) * half]
    gate = jax.nn.sigmoid(project(3) + offset_ref[...])
    lane_head = lax.broadcasted_iota(jnp.int32, (1, width), 1) // depth
    side = heads // 2
    for h in range(heads):
        own = (lane_head == h).astype(F32).astype(BF16)
        ones = (lane_head == (h + side) % heads).astype(F32).astype(BF16)
        keys = k_ref[...].reshape(length, width) * own
        values = v_ref[...].reshape(length, width) * own + ones
        mixed_ref = mixed_refs[h // side]
        rows = max(block_rows, length // 2)
        for t in range(0, length, rows):
            scores = lax.dot_general(
                q_ref[t : t + rows], keys, ROWS_BY_ROWS, preferred_element_type=F32
            )
            first, count = t // block_rows, rows // block_rows
            bias = jnp.concatenate(
                [
                    jnp.concatenate(
                        [b[place_ref[1 + first + p], h] for p in range(count)], axis=0
                    )
                    for b in biases
                ],
                axis=1,
            )
            scores = scores + bias.astype(F32)
            exponent = jnp.exp(scores - jnp.max(scores, axis=-1, keepdims=True)).astype(BF16)
            mixed = jnp.dot(exponent, values, preferred_element_type=F32)
            if h % side == 0:
                mixed_ref[t : t + rows] = mixed
            else:
                mixed_ref[t : t + rows] += mixed
    middle = side * depth
    mixed = jnp.concatenate(
        [
            mixed_refs[0][:, :middle] / mixed_refs[0][:, middle:],
            mixed_refs[1][:, middle:] / mixed_refs[1][:, :middle],
        ],
        axis=1,
    )
    gated = (mixed * gate).astype(BF16)
    stream = x + jnp.dot(gated, final_ref[...], preferred_element_type=F32)
    normed = layer_normalize(stream, gain2_ref[...]).astype(BF16)
    hidden = jnp.maximum(
        jnp.dot(normed, widen_ref[...], preferred_element_type=F32), 0.0
    ).astype(BF16)
    updated = (stream + jnp.dot(hidden, shrink_ref[...], preferred_element_type=F32)).astype(BF16)
    out_ref[:, 0] = updated.reshape(blocks, block_rows, width)
    normed = layer_normalize(updated.astype(F32), gain3_ref[...]).astype(BF16)
    factors = lax.dot_general(
        twin_ref[...], normed, ROWS_BY_ROWS, preferred_element_type=F32
    ).astype(BF16)
    for j in range(halves):
        right_ref[lax.rem(j + halves - seq, halves), 0] = factors[:, j * half : (j + 1) * half]


def attend(place, x, first, seqs, biases, params, heads):
    halves = len(biases)
    blocks, _, block_rows, width = x.shape
    length = blocks * block_rows
    half = length // halves
    factor_width = params[-1].shape[0]
    hidden = params[5].shape[1]
    held = tuple(biases) + params

    def whole(array):
        return pl.BlockSpec(array.shape, lambda s, place: (0,) * array.ndim)

    flops = 2 * seqs * (
        2 * length * width * (5 * width + 2 * hidden + factor_width)
        + 4 * heads * length * length * width
    )
    block = (blocks, 1, block_rows, width)
    return pl.pallas_call(
        functools.partial(attend_kernel, heads, blocks, halves),
        grid_spec=pltpu.PrefetchScalarGridSpec(
            num_scalar_prefetch=1,
            grid=(seqs,),
            in_specs=[pl.BlockSpec(block, lambda s, place: (0, first + s, 0, 0))]
            + [whole(array) for array in held],
            out_specs=[
                pl.BlockSpec(block, lambda s, place: (0, s, 0, 0)),
                pl.BlockSpec((halves, 1, factor_width, half), lambda s, place: (0, s, 0, 0)),
            ],
            scratch_shapes=[
                pltpu.VMEM((length, width), BF16),
                pltpu.VMEM((halves, half, width), BF16),
                pltpu.VMEM((halves, half, width), BF16),
                pltpu.VMEM((length, width), F32),
                pltpu.VMEM((length, width), F32),
            ],
        ),
        out_shape=[
            jax.ShapeDtypeStruct((blocks, seqs, block_rows, width), BF16),
            jax.ShapeDtypeStruct((halves, seqs, factor_width, half), BF16),
        ],
        compiler_params=pltpu.CompilerParams(vmem_limit_bytes=VMEM_BYTES),
        cost_estimate=pl.CostEstimate(
            flops=flops,
            bytes_accessed=4 * seqs * length * width + 2 * heads * length * length,
            transcendentals=seqs * heads * length * length,
        ),
        name="attend",
    )(place, x, *held)


def bias_kernel(pair_ref, gain_ref, matrix_ref, out_ref, held_ref):
    for i in range(pair_ref.shape[0]):
        normed = layer_normalize(pair_ref[i].astype(F32), gain_ref[...])
        held_ref[:, i, :] = lax.dot_general(
            matrix_ref[...],
            normed,
            ROWS_BY_ROWS,
            precision=lax.Precision.HIGHEST,
            preferred_element_type=F32,
        )
    out_ref[...] = held_ref[...].astype(BF16)


def head_biases(pair_state, gain, matrix):
    row_count, cols, channels = pair_state.shape
    heads = matrix.shape[1]
    rows = math.gcd(row_count, 16)
    return pl.pallas_call(
        bias_kernel,
        grid=(row_count // rows,),
        in_specs=[
            pl.BlockSpec((rows, cols, channels), lambda i: (i, 0, 0)),
            pl.BlockSpec((1, channels), lambda i: (0, 0)),
            pl.BlockSpec((heads, channels), lambda i: (0, 0)),
        ],
        out_specs=pl.BlockSpec((heads, rows, cols), lambda i: (0, i, 0)),
        out_shape=jax.ShapeDtypeStruct((heads, row_count, cols), BF16),
        scratch_shapes=[pltpu.VMEM((heads, rows, cols), F32)],
        compiler_params=pltpu.CompilerParams(vmem_limit_bytes=VMEM_BYTES),
        cost_estimate=pl.CostEstimate(
            flops=100 * pair_state.size, bytes_accessed=2 * pair_state.size, transcendentals=0
        ),
        name="head_biases",
    )(pair_state, gain.reshape(1, -1), matrix.T)


def left_kernel(place_ref, x_ref, gain_ref, twin_ref, out_ref):
    blocks, seqs, rows, width = x_ref.shape
    x = jnp.concatenate([x_ref[place_ref[k]] for k in range(blocks)], axis=0)
    normed = layer_normalize(x.reshape(blocks * seqs * rows, width).astype(F32), gain_ref[...])
    out_ref[...] = lax.dot_general(
        twin_ref[...], normed.astype(BF16), ROWS_BY_ROWS, preferred_element_type=F32
    ).astype(BF16)


def left_factors(origins, x, gain, twin):
    blocks, seqs, rows, width = x.shape

    def whole(array):
        return pl.BlockSpec(array.shape, lambda i, place: (0,) * array.ndim)

    total = blocks * seqs * rows
    return pl.pallas_call(
        left_kernel,
        grid_spec=pltpu.PrefetchScalarGridSpec(
            num_scalar_prefetch=1,
            grid=(1,),
            in_specs=[whole(x), whole(gain), whole(twin)],
            out_specs=pl.BlockSpec((twin.shape[0], total), lambda i, place: (0, 0)),
        ),
        out_shape=jax.ShapeDtypeStruct((twin.shape[0], total), BF16),
        compiler_params=pltpu.CompilerParams(vmem_limit_bytes=VMEM_BYTES),
        cost_estimate=pl.CostEstimate(
            flops=8 * x.size * twin.shape[0], bytes_accessed=2 * x.size, transcendentals=0
        ),
        name="left_factors",
    )(origins, x, gain, twin)


def outer_kernel(rows, seq_total, left_ref, right_ref, final_ref, pair_ref, out_ref, mean_ref):
    width = right_ref.shape[0]
    left = left_ref[...]
    for e in range(width):
        outer = jnp.dot(left, right_ref[e], preferred_element_type=F32).astype(BF16)
        mean_ref[:, e * width : (e + 1) * width, :] = outer.reshape(rows, width, -1)
    final = final_ref[...]
    for i in range(rows):
        update = jnp.dot(final, mean_ref[i], preferred_element_type=F32)
        out_ref[i] = (pair_ref[i].astype(F32) + update.T * (1.0 / seq_total)).astype(BF16)


def outer_update(left, right, final, pair_state):
    width, seqs, cols = right.shape
    row_count, _, channels = pair_state.shape
    rows = math.gcd(row_count, 16)

    def whole(array):
        return pl.BlockSpec(array.shape, lambda i: (0,) * array.ndim)

    block = pl.BlockSpec((rows, cols, channels), lambda i: (i, 0, 0))
    return pl.pallas_call(
        functools.partial(outer_kernel, rows, float(seqs)),
        grid=(row_count // rows,),
        in_specs=[
            pl.BlockSpec((rows * width, seqs), lambda i: (i, 0)),
            whole(right),
            whole(final),
            block,
        ],
        out_specs=block,
        out_shape=jax.ShapeDtypeStruct(pair_state.shape, BF16),
        scratch_shapes=[pltpu.VMEM((rows, width * width, cols), BF16)],
        compiler_params=pltpu.CompilerParams(vmem_limit_bytes=VMEM_BYTES),
        cost_estimate=pl.CostEstimate(
            flops=2 * row_count * width * width * cols * (seqs + channels),
            bytes_accessed=2 * right.size + 4 * pair_state.size,
            transcendentals=0,
        ),
        name="outer_update",
    )(left, right, final, pair_state)


def on_device(
    aligned_activity,
    pair_state,
    focus_scaling_vector,
    combined_probe_matrix,
    sigmoid_offset_vector,
    focus_final_matrix,
    pair_norm_gain,
    pair_bias_matrix,
    feedforward_scaling_vector,
    feedforward_widen_matrix,
    feedforward_shrink_matrix,
    tensor_scaling_vector,
    twin_operand_matrix,
    tensor_final_matrix,
):
    factor_width = twin_operand_matrix.shape[1] // 2
    heads = pair_bias_matrix.shape[1]
    channels = tensor_final_matrix.shape[1]
    seq_local, res_local, width = aligned_activity.shape
    blocks = lax.axis_size("res")
    halves = lax.axis_size("seq")
    res = lax.axis_index("res")
    seq = lax.axis_index("seq")
    chunks = math.gcd(seq_local // blocks, CHUNKS)
    seqs = seq_local // blocks // chunks
    joined = [1, chunks - 1] if chunks > 1 else [1]
    early = max(0, chunks - 2)
    near = math.gcd(blocks, NEAR)
    far = blocks // near

    def after(value, *done):
        return lax.optimization_barrier((value, done))[0]

    def from_cores(own, sent):
        return [own] + [
            lax.ppermute(sent(k), "seq", [(i, (i + k) % halves) for i in range(halves)])
            for k in range(1, halves)
        ]

    def far_gather(block):
        return [block] + [
            lax.ppermute(block, "res", [(i, (i + k * near) % blocks) for i in range(blocks)])
            for k in range(1, far)
        ]

    def near_gather(listed, each):
        lists = listed if each else [jnp.stack(listed)]
        for k in range(1, near):
            moves = [(i, i - i % near + (i + k) % near) for i in range(blocks)]
            lists = lists + [lax.ppermute(part, "res", moves) for part in lists]
        return jnp.stack(lists) if each else jnp.concatenate(lists)

    close, away = jnp.arange(near)[:, None], jnp.arange(far)[None, :]
    origins = (res // near - away) % far * near + (res % near - close) % near
    origins = origins.reshape(-1).astype(jnp.int32)
    p = jnp.arange(blocks)
    slots = (res % near - p % near) % near * far + (res // near - p // near) % far
    place = jnp.concatenate([seq.reshape(1), slots]).astype(jnp.int32)

    tile = head_biases(pair_state, pair_norm_gain, pair_bias_matrix)
    far_bias = far_gather(tile)
    arrivals, sources = [], []
    start = 0
    for size in joined:
        rows = blocks * seqs * size
        part = aligned_activity[start : start + rows]
        part = part.reshape(blocks, seqs * size, res_local, width)
        start += rows
        if arrivals:
            part = after(part, arrivals[-1], far_bias)
        arrivals.append(lax.all_to_all(part, "res", 0, 0))
        sources += [(len(arrivals) - 1, k * seqs) for k in range(size)]

    bias = after(near_gather(far_bias, True), arrivals[0])
    biases = from_cores(bias, lambda k: bias)
    biases = biases[:1] + biases[:0:-1]

    gain3 = tensor_scaling_vector.reshape(1, -1)
    params = (
        focus_scaling_vector.reshape(1, -1),
        combined_probe_matrix,
        sigmoid_offset_vector.reshape(1, -1),
        focus_final_matrix,
        feedforward_scaling_vector.reshape(1, -1),
        feedforward_widen_matrix,
        feedforward_shrink_matrix,
        gain3,
        twin_operand_matrix[:, factor_width:].T,
    )
    left_twin = twin_operand_matrix[:, :factor_width].T
    natural = jnp.arange(blocks, dtype=jnp.int32)
    outputs, lefts, rights, gathered, pending = [], [], [], [], None

    def swap(listed):
        return jnp.stack(from_cores(listed[:, 0], lambda k: listed[:, k]), axis=1)

    def finish(c):
        order = natural if c < early else origins
        left = left_factors(order, outputs[c], gain3, left_twin)
        left = left.reshape(factor_width, blocks, seqs, res_local)
        lefts.append(left.transpose(3, 0, 1, 2).reshape(res_local * factor_width, blocks, seqs))

    for c in range(chunks):
        done = []
        if c >= 1:
            done += [arrivals[-1]]
        if c >= 2:
            done += [outputs[c - 2]]
            finish(c - 2)
            done += [lefts[c - 2]]
        source, first = sources[c]
        updated, right = attend(
            after(place, *done), arrivals[source], first, seqs, biases, params, heads
        )
        updated = after(updated, outputs[-1] if outputs else arrivals[-1])
        outputs.append(lax.all_to_all(updated, "res", 0, 0))
        rights.append(right)
        if c + 1 == early:
            gathered.append(lax.all_gather(jnp.concatenate(rights, axis=1), "res"))
        elif c >= early:
            if pending is not None:
                gathered.append(near_gather(after(pending, right), False))
            pending = far_gather(after(right, outputs[c - 1]) if c == chunks - 1 > 0 else right)
    gathered.append(near_gather(after(pending, outputs[-1]), False))
    if early:
        gathered[0] = after(gathered[0], outputs[-2])
    for c in range(max(0, chunks - 2), chunks):
        finish(c)

    rights = [swap(listed) for listed in gathered]
    right = jnp.concatenate([r.reshape(-1, *r.shape[3:]) for r in rights]).transpose(1, 0, 2)
    left = jnp.concatenate(lefts, axis=2)
    left = jnp.stack(from_cores(left, lambda k: left), axis=2)
    groups, start = [], 0
    for r in rights:
        part = left[..., start : start + r.shape[2]]
        start += r.shape[2]
        groups.append(part.reshape(res_local * factor_width, -1))
    left = jnp.concatenate(groups, axis=1)
    final = tensor_final_matrix.reshape(factor_width, factor_width, channels)
    final = final.transpose(2, 1, 0).reshape(channels, -1)
    pair_output = outer_update(left, right, final, pair_state)
    output = []
    for c in range(len(joined)):
        group = [outputs[k] for k, source in enumerate(sources) if source[0] == c]
        output.append(jnp.concatenate(group, axis=1).reshape(-1, res_local, width))
    output = jnp.concatenate(output)
    return (output, pair_output)


def solution(mesh):
    return jax.shard_map(
        on_device,
        mesh=mesh,
        in_specs=(
            P(("grp", "seq"), "res", None),
            P(("grp", "res"), "seq", None),
        )
        + (P(),) * 12,
        out_specs=(P(("grp", "seq"), "res", None), P(("grp", "res"), "seq", None)),
        check_vma=False,
    )
```

```python
import functools
import math

import jax
import jax.numpy as jnp
from jax import lax
from jax.experimental import pallas as pl
from jax.experimental.pallas import tpu as pltpu
from jax.sharding import PartitionSpec as P

CHUNKS = 4
NEAR = 2
VMEM_BYTES = 56 * 2**20
F32 = jnp.float32
BF16 = jnp.bfloat16
ROWS_BY_ROWS = (((1,), (1,)), ((), ()))


def layer_normalize(inputs, scale_gain):
    sample_expectation = jnp.mean(inputs, axis=-1, keepdims=True)
    centered = inputs - sample_expectation
    variance = jnp.mean(centered * centered, axis=-1, keepdims=True)
    return centered * lax.rsqrt(variance + 1e-05) * scale_gain


def attend_kernel(heads, blocks, halves, place_ref, *refs):
    x_ref, refs = refs[0], refs[1:]
    biases, refs = refs[:halves], refs[halves:]
    (gain1_ref, probe_ref, offset_ref, final_ref, gain2_ref, widen_ref, shrink_ref) = refs[:7]
    (gain3_ref, twin_ref, out_ref, right_ref) = refs[7:11]
    q_ref, k_ref, v_ref = refs[11:14]
    mixed_refs = refs[14:16]
    late, refs = refs[16:-1], refs[-1]
    copies = [
        pltpu.make_async_copy(source, target, refs.at[i])
        for i, (source, target) in enumerate(zip((*biases, widen_ref, shrink_ref), late))
    ]
    *biases, widen_ref, shrink_ref = late

    @pl.when(pl.program_id(0) == 0)
    def _():
        for copy in copies:
            copy.start()

    _, _, block_rows, width = x_ref.shape
    length = blocks * block_rows
    depth = width // heads
    half = length // halves
    seq = place_ref[0]
    x = x_ref[:, 0].reshape(length, width).astype(F32)
    normed = layer_normalize(x, gain1_ref[...]).astype(BF16)

    def project(part):
        return jnp.dot(
            normed, probe_ref[:, part * width : (part + 1) * width], preferred_element_type=F32
        )

    q_ref[...] = (project(0) * depth**-0.5).astype(BF16)
    for held, part in ((k_ref, 1), (v_ref, 2)):
        rows = project(part).astype(BF16)
        for j in range(halves):
            slot = lax.rem(j + halves - seq, halves)
            held[slot] = rows[j * half : (j + 1) * half]
    gate = jax.nn.sigmoid(project(3) + offset_ref[...])

    @pl.when(pl.program_id(0) == 0)
    def _():
        for copy in copies:
            copy.wait()

    lane_head = lax.broadcasted_iota(jnp.int32, (1, width), 1) // depth
    side = heads // 2
    for h in range(heads):
        own = (lane_head == h).astype(F32).astype(BF16)
        ones = (lane_head == (h + side) % heads).astype(F32).astype(BF16)
        keys = k_ref[...].reshape(length, width) * own
        values = v_ref[...].reshape(length, width) * own + ones
        mixed_ref = mixed_refs[h // side]
        rows = max(block_rows, length // 2)
        for t in range(0, length, rows):
            scores = lax.dot_general(
                q_ref[t : t + rows], keys, ROWS_BY_ROWS, preferred_element_type=F32
            )
            first, count = t // block_rows, rows // block_rows
            bias = jnp.concatenate(
                [
                    jnp.concatenate(
                        [b[place_ref[1 + first + p], h] for p in range(count)], axis=0
                    )
                    for b in biases
                ],
                axis=1,
            )
            scores = scores + bias.astype(F32)
            exponent = jnp.exp(scores - jnp.max(scores, axis=-1, keepdims=True)).astype(BF16)
            mixed = jnp.dot(exponent, values, preferred_element_type=F32)
            if h % side == 0:
                mixed_ref[t : t + rows] = mixed
            else:
                mixed_ref[t : t + rows] += mixed
    middle = side * depth
    mixed = jnp.concatenate(
        [
            mixed_refs[0][:, :middle] / mixed_refs[0][:, middle:],
            mixed_refs[1][:, middle:] / mixed_refs[1][:, :middle],
        ],
        axis=1,
    )
    gated = (mixed * gate).astype(BF16)
    stream = x + jnp.dot(gated, final_ref[...], preferred_element_type=F32)
    normed = layer_normalize(stream, gain2_ref[...]).astype(BF16)
    hidden = jnp.maximum(
        jnp.dot(normed, widen_ref[...], preferred_element_type=F32), 0.0
    ).astype(BF16)
    updated = (stream + jnp.dot(hidden, shrink_ref[...], preferred_element_type=F32)).astype(BF16)
    out_ref[:, 0] = updated.reshape(blocks, block_rows, width)
    normed = layer_normalize(updated.astype(F32), gain3_ref[...]).astype(BF16)
    factors = lax.dot_general(
        twin_ref[...], normed, ROWS_BY_ROWS, preferred_element_type=F32
    ).astype(BF16)
    for j in range(halves):
        right_ref[lax.rem(j + halves - seq, halves), 0] = factors[:, j * half : (j + 1) * half]


def attend(place, x, first, seqs, biases, params, heads):
    halves = len(biases)
    blocks, _, block_rows, width = x.shape
    length = blocks * block_rows
    half = length // halves
    factor_width = params[-1].shape[0]
    hidden = params[5].shape[1]
    held = tuple(biases) + params
    late = tuple(biases) + params[5:7]
    in_place = pl.BlockSpec(memory_space=pl.ANY)

    def whole(array):
        return pl.BlockSpec(array.shape, lambda s, place: (0,) * array.ndim)

    flops = 2 * seqs * (
        2 * length * width * (5 * width + 2 * hidden + factor_width)
        + 4 * heads * length * length * width
    )
    block = (blocks, 1, block_rows, width)
    return pl.pallas_call(
        functools.partial(attend_kernel, heads, blocks, halves),
        grid_spec=pltpu.PrefetchScalarGridSpec(
            num_scalar_prefetch=1,
            grid=(seqs,),
            in_specs=[pl.BlockSpec(block, lambda s, place: (0, first + s, 0, 0))]
            + [in_place] * halves
            + [whole(array) for array in params[:5]]
            + [in_place] * 2
            + [whole(array) for array in params[7:]],
            out_specs=[
                pl.BlockSpec(block, lambda s, place: (0, s, 0, 0)),
                pl.BlockSpec((halves, 1, factor_width, half), lambda s, place: (0, s, 0, 0)),
            ],
            scratch_shapes=[
                pltpu.VMEM((length, width), BF16),
                pltpu.VMEM((halves, half, width), BF16),
                pltpu.VMEM((halves, half, width), BF16),
                pltpu.VMEM((length, width), F32),
                pltpu.VMEM((length, width), F32),
            ]
            + [pltpu.VMEM(array.shape, array.dtype) for array in late]
            + [pltpu.SemaphoreType.DMA((len(late),))],
        ),
        out_shape=[
            jax.ShapeDtypeStruct((blocks, seqs, block_rows, width), BF16),
            jax.ShapeDtypeStruct((halves, seqs, factor_width, half), BF16),
        ],
        compiler_params=pltpu.CompilerParams(vmem_limit_bytes=VMEM_BYTES),
        cost_estimate=pl.CostEstimate(
            flops=flops,
            bytes_accessed=4 * seqs * length * width + 2 * heads * length * length,
            transcendentals=seqs * heads * length * length,
        ),
        name="attend",
    )(place, x, *held)


def bias_kernel(pair_ref, gain_ref, matrix_ref, out_ref, held_ref):
    for i in range(pair_ref.shape[0]):
        normed = layer_normalize(pair_ref[i].astype(F32), gain_ref[...])
        held_ref[:, i, :] = lax.dot_general(
            matrix_ref[...],
            normed,
            ROWS_BY_ROWS,
            precision=lax.Precision.HIGHEST,
            preferred_element_type=F32,
        )
    out_ref[...] = held_ref[...].astype(BF16)


def head_biases(pair_state, gain, matrix):
    row_count, cols, channels = pair_state.shape
    heads = matrix.shape[1]
    rows = math.gcd(row_count, 16)
    return pl.pallas_call(
        bias_kernel,
        grid=(row_count // rows,),
        in_specs=[
            pl.BlockSpec((rows, cols, channels), lambda i: (i, 0, 0)),
            pl.BlockSpec((1, channels), lambda i: (0, 0)),
            pl.BlockSpec((heads, channels), lambda i: (0, 0)),
        ],
        out_specs=pl.BlockSpec((heads, rows, cols), lambda i: (0, i, 0)),
        out_shape=jax.ShapeDtypeStruct((heads, row_count, cols), BF16),
        scratch_shapes=[pltpu.VMEM((heads, rows, cols), F32)],
        compiler_params=pltpu.CompilerParams(vmem_limit_bytes=VMEM_BYTES),
        cost_estimate=pl.CostEstimate(
            flops=100 * pair_state.size, bytes_accessed=2 * pair_state.size, transcendentals=0
        ),
        name="head_biases",
    )(pair_state, gain.reshape(1, -1), matrix.T)


def left_kernel(place_ref, x_ref, gain_ref, twin_ref, out_ref):
    blocks, seqs, rows, width = x_ref.shape
    x = jnp.concatenate([x_ref[place_ref[k]] for k in range(blocks)], axis=0)
    normed = layer_normalize(x.reshape(blocks * seqs * rows, width).astype(F32), gain_ref[...])
    out_ref[...] = lax.dot_general(
        twin_ref[...], normed.astype(BF16), ROWS_BY_ROWS, preferred_element_type=F32
    ).astype(BF16)


def left_factors(origins, x, gain, twin):
    blocks, seqs, rows, width = x.shape

    def whole(array):
        return pl.BlockSpec(array.shape, lambda i, place: (0,) * array.ndim)

    total = blocks * seqs * rows
    return pl.pallas_call(
        left_kernel,
        grid_spec=pltpu.PrefetchScalarGridSpec(
            num_scalar_prefetch=1,
            grid=(1,),
            in_specs=[whole(x), whole(gain), whole(twin)],
            out_specs=pl.BlockSpec((twin.shape[0], total), lambda i, place: (0, 0)),
        ),
        out_shape=jax.ShapeDtypeStruct((twin.shape[0], total), BF16),
        compiler_params=pltpu.CompilerParams(vmem_limit_bytes=VMEM_BYTES),
        cost_estimate=pl.CostEstimate(
            flops=8 * x.size * twin.shape[0], bytes_accessed=2 * x.size, transcendentals=0
        ),
        name="left_factors",
    )(origins, x, gain, twin)


def outer_kernel(rows, seq_total, left_ref, right_ref, final_ref, pair_ref, out_ref, mean_ref):
    width = right_ref.shape[0]
    left = left_ref[...]
    for e in range(width):
        outer = jnp.dot(left, right_ref[e], preferred_element_type=F32).astype(BF16)
        mean_ref[:, e * width : (e + 1) * width, :] = outer.reshape(rows, width, -1)
    final = final_ref[...]
    for i in range(rows):
        update = jnp.dot(final, mean_ref[i], preferred_element_type=F32)
        out_ref[i] = (pair_ref[i].astype(F32) + update.T * (1.0 / seq_total)).astype(BF16)


def outer_update(left, right, final, pair_state):
    width, seqs, cols = right.shape
    row_count, _, channels = pair_state.shape
    rows = math.gcd(row_count, 16)

    def whole(array):
        return pl.BlockSpec(array.shape, lambda i: (0,) * array.ndim)

    block = pl.BlockSpec((rows, cols, channels), lambda i: (i, 0, 0))
    return pl.pallas_call(
        functools.partial(outer_kernel, rows, float(seqs)),
        grid=(row_count // rows,),
        in_specs=[
            pl.BlockSpec((rows * width, seqs), lambda i: (i, 0)),
            whole(right),
            whole(final),
            block,
        ],
        out_specs=block,
        out_shape=jax.ShapeDtypeStruct(pair_state.shape, BF16),
        scratch_shapes=[pltpu.VMEM((rows, width * width, cols), BF16)],
        compiler_params=pltpu.CompilerParams(vmem_limit_bytes=VMEM_BYTES),
        cost_estimate=pl.CostEstimate(
            flops=2 * row_count * width * width * cols * (seqs + channels),
            bytes_accessed=2 * right.size + 4 * pair_state.size,
            transcendentals=0,
        ),
        name="outer_update",
    )(left, right, final, pair_state)


def on_device(
    aligned_activity,
    pair_state,
    focus_scaling_vector,
    combined_probe_matrix,
    sigmoid_offset_vector,
    focus_final_matrix,
    pair_norm_gain,
    pair_bias_matrix,
    feedforward_scaling_vector,
    feedforward_widen_matrix,
    feedforward_shrink_matrix,
    tensor_scaling_vector,
    twin_operand_matrix,
    tensor_final_matrix,
):
    factor_width = twin_operand_matrix.shape[1] // 2
    heads = pair_bias_matrix.shape[1]
    channels = tensor_final_matrix.shape[1]
    seq_local, res_local, width = aligned_activity.shape
    blocks = lax.axis_size("res")
    halves = lax.axis_size("seq")
    res = lax.axis_index("res")
    seq = lax.axis_index("seq")
    chunks = math.gcd(seq_local // blocks, CHUNKS)
    seqs = seq_local // blocks // chunks
    joined = [1, chunks - 1] if chunks > 1 else [1]
    early = max(0, chunks - 2)
    near = math.gcd(blocks, NEAR)
    far = blocks // near

    def after(value, *done):
        return lax.optimization_barrier((value, done))[0]

    def from_cores(own, sent):
        return [own] + [
            lax.ppermute(sent(k), "seq", [(i, (i + k) % halves) for i in range(halves)])
            for k in range(1, halves)
        ]

    def far_gather(block):
        return [block] + [
            lax.ppermute(block, "res", [(i, (i + k * near) % blocks) for i in range(blocks)])
            for k in range(1, far)
        ]

    def near_gather(listed, each):
        lists = listed if each else [jnp.stack(listed)]
        for k in range(1, near):
            moves = [(i, i - i % near + (i + k) % near) for i in range(blocks)]
            lists = lists + [lax.ppermute(part, "res", moves) for part in lists]
        return jnp.stack(lists) if each else jnp.concatenate(lists)

    close, away = jnp.arange(near)[:, None], jnp.arange(far)[None, :]
    origins = (res // near - away) % far * near + (res % near - close) % near
    origins = origins.reshape(-1).astype(jnp.int32)
    p = jnp.arange(blocks)
    slots = (res % near - p % near) % near * far + (res // near - p // near) % far
    place = jnp.concatenate([seq.reshape(1), slots]).astype(jnp.int32)

    tile = head_biases(pair_state, pair_norm_gain, pair_bias_matrix)
    far_bias = far_gather(tile)
    arrivals, sources = [], []
    start = 0
    for size in joined:
        rows = blocks * seqs * size
        part = aligned_activity[start : start + rows]
        part = part.reshape(blocks, seqs * size, res_local, width)
        start += rows
        if arrivals:
            part = after(part, arrivals[-1], far_bias)
        arrivals.append(lax.all_to_all(part, "res", 0, 0))
        sources += [(len(arrivals) - 1, k * seqs) for k in range(size)]

    bias = after(near_gather(far_bias, True), arrivals[0])
    biases = from_cores(bias, lambda k: bias)
    biases = biases[:1] + biases[:0:-1]

    gain3 = tensor_scaling_vector.reshape(1, -1)
    params = (
        focus_scaling_vector.reshape(1, -1),
        combined_probe_matrix,
        sigmoid_offset_vector.reshape(1, -1),
        focus_final_matrix,
        feedforward_scaling_vector.reshape(1, -1),
        feedforward_widen_matrix,
        feedforward_shrink_matrix,
        gain3,
        twin_operand_matrix[:, factor_width:].T,
    )
    left_twin = twin_operand_matrix[:, :factor_width].T
    natural = jnp.arange(blocks, dtype=jnp.int32)
    outputs, lefts, rights, gathered, pending = [], [], [], [], None

    def swap(listed):
        return jnp.stack(from_cores(listed[:, 0], lambda k: listed[:, k]), axis=1)

    def finish(c):
        order = natural if c < early else origins
        left = left_factors(order, outputs[c], gain3, left_twin)
        left = left.reshape(factor_width, blocks, seqs, res_local)
        lefts.append(left.transpose(3, 0, 1, 2).reshape(res_local * factor_width, blocks, seqs))

    for c in range(chunks):
        done = []
        if c >= 1:
            done += [arrivals[-1]]
        if c >= 2:
            done += [outputs[c - 2]]
            finish(c - 2)
            done += [lefts[c - 2]]
        source, first = sources[c]
        updated, right = attend(
            after(place, *done), arrivals[source], first, seqs, biases, params, heads
        )
        updated = after(updated, outputs[-1] if outputs else arrivals[-1])
        outputs.append(lax.all_to_all(updated, "res", 0, 0))
        rights.append(right)
        if c + 1 == early:
            gathered.append(lax.all_gather(jnp.concatenate(rights, axis=1), "res"))
        elif c >= early:
            if pending is not None:
                gathered.append(near_gather(after(pending, right), False))
            pending = far_gather(after(right, outputs[c - 1]) if c == chunks - 1 > 0 else right)
    gathered.append(near_gather(after(pending, outputs[-1]), False))
    if early:
        gathered[0] = after(gathered[0], outputs[-2])
    for c in range(max(0, chunks - 2), chunks):
        finish(c)

    rights = [swap(listed) for listed in gathered]
    right = jnp.concatenate([r.reshape(-1, *r.shape[3:]) for r in rights]).transpose(1, 0, 2)
    left = jnp.concatenate(lefts, axis=2)
    left = jnp.stack(from_cores(left, lambda k: left), axis=2)
    groups, start = [], 0
    for r in rights:
        part = left[..., start : start + r.shape[2]]
        start += r.shape[2]
        groups.append(part.reshape(res_local * factor_width, -1))
    left = jnp.concatenate(groups, axis=1)
    final = tensor_final_matrix.reshape(factor_width, factor_width, channels)
    final = final.transpose(2, 1, 0).reshape(channels, -1)
    pair_output = outer_update(left, right, final, pair_state)
    output = []
    for c in range(len(joined)):
        group = [outputs[k] for k, source in enumerate(sources) if source[0] == c]
        output.append(jnp.concatenate(group, axis=1).reshape(-1, res_local, width))
    output = jnp.concatenate(output)
    return (output, pair_output)


def solution(mesh):
    return jax.shard_map(
        on_device,
        mesh=mesh,
        in_specs=(
            P(("grp", "seq"), "res", None),
            P(("grp", "res"), "seq", None),
        )
        + (P(),) * 12,
        out_specs=(P(("grp", "seq"), "res", None), P(("grp", "res"), "seq", None)),
        check_vma=False,
    )
```
